32 devices in a mesh: ctx: 4 (over y, x), tp: 8 (over z, core).
Axes of the slice: x: 2, y: 2, z: 4, core: 2. Of those that a mesh axis runs over, the one named last changes fastest.
Arguments:
- tokens: bfloat16 [4096, 2560], P(('ctx', 'tp')), may hold values from -8 to 8
- norm1_gain: float32 [2560], replicated, may hold values from 0.1 to 1.9
- w_z: bfloat16 [2560, 5120], P(None, 'tp'), may hold values from -0.125 to 0.125
- w_x: bfloat16 [2560, 5120], P(None, 'tp'), may hold values from -0.125 to 0.125
- w_bc: bfloat16 [2560, 256], replicated, may hold values from -0.125 to 0.125
- w_dt: bfloat16 [2560, 80], P(None, 'tp'), may hold values from -1 to 1
- dt_bias: float32 [80], P('tp'), may hold values from -5.5 to -4
- a_log: float32 [80], P('tp'), may hold values from -12 to 1.4
- conv_x: float32 [4, 5120], P(None, 'tp'), may hold values from -3 to 3
- conv_bc: float32 [4, 256], replicated, may hold values from -3 to 3
- d_skip: float32 [80], P('tp'), may hold values from 0.1 to 1.9
- ssm_gain: float32 [5120], P('tp'), may hold values from 0.1 to 1.9
- w_out: bfloat16 [5120, 2560], P('tp'), may hold values from -0.078125 to 0.078125
- norm2_gain: float32 [2560], replicated, may hold values from 0.1 to 1.9
- w_gate: bfloat16 [2560, 5120], P(None, 'tp'), may hold values from -0.125 to 0.125
- w_up: bfloat16 [2560, 5120], P(None, 'tp'), may hold values from -0.125 to 0.125
- w_down: bfloat16 [5120, 2560], P('tp'), may hold values from -0.078125 to 0.078125
Outputs:
- layer_out: bfloat16 [4096, 2560], P(('ctx', 'tp'))
The draws below stay inside these ranges and needn't reach their ends.
All inputs are finite; a program needn't handle non-finite values.
Results may differ from the reference program's by a relative error of at most 0.017.
Values may be sent and summed in bfloat16 or wider, within the bound.
A program may use at most 128 MiB of HBM per device.

```python
import math
import jax
import jax.numpy as jnp
from jax import lax

WIDTH = 2560
HEADS = 80
HEAD_DIM = 64
STATE_DIM = 128
MLP_DIM = 5120
BLOCK_LEN = 256
TOK_DEV = 1024
SEQ_LEN = 4096
N_TP = 8


def draw_a_log(key, part):
    key_pick, key_fast, key_slow = jax.random.split(key, 3)
    share = 0.5
    picker = jax.random.uniform(key_pick, (HEADS,), dtype=jnp.float32)
    fast_rate = jnp.exp(jax.random.uniform(key_fast, (HEADS,), dtype=jnp.float32, minval=math.log(1.5), maxval=math.log(4.0)))
    slow_rate = jax.random.uniform(key_slow, (HEADS,), dtype=jnp.float32, minval=0.05, maxval=1.0) * (100.0 / SEQ_LEN)
    chosen = jnp.where(picker < share, fast_rate, slow_rate)
    return jnp.log(chosen).astype(jnp.float32)


def common_direction(key):
    raw = jax.random.normal(jax.random.fold_in(key, 7), (WIDTH,), dtype=jnp.float32)
    return raw * lax_rsqrt_sum(raw)


def lax_rsqrt_sum(raw):
    return 1.0 / jnp.sqrt(jnp.sum(raw * raw))


def draw_w_dt(key, part):
    direction = common_direction(key)
    noise = jax.random.normal(jax.random.fold_in(key, 11), (WIDTH, HEADS), dtype=jnp.float32) / math.sqrt(WIDTH)
    loads = jax.random.uniform(jax.random.fold_in(key, 19), (HEADS,), dtype=jnp.float32, minval=-3.0, maxval=3.0) / math.sqrt(WIDTH)
    result = noise + direction[:, None] * loads[None, :]
    return jnp.clip(result, -1.0, 1.0).astype(jnp.bfloat16)


def draw_tokens(key, part):
    direction = common_direction(key)
    noise = jax.random.normal(jax.random.fold_in(key, 13), (SEQ_LEN, WIDTH), dtype=jnp.float32)
    group_shift = jax.random.uniform(jax.random.fold_in(key, 17), (SEQ_LEN // TOK_DEV,), dtype=jnp.float32, minval=-3.0, maxval=3.0)
    per_row = jnp.repeat(group_shift, TOK_DEV)
    result = noise + per_row[:, None] * (math.sqrt(WIDTH) * direction)[None, :]
    return jnp.clip(result, -8.0, 8.0).astype(jnp.bfloat16)


def levels(stream_key, extent, cuts, least, high):
    def one(axis_at, parts):
        heights = jax.random.uniform(jax.random.fold_in(jax.random.fold_in(stream_key, 6), axis_at), (parts,), jnp.float32, least / len(cuts), high / len(cuts))
        return jnp.repeat(jnp.exp(heights), extent[axis_at] // parts).reshape((-1,) + (1,) * (len(extent) - axis_at - 1))

    level = one(*cuts[0])
    for cut in cuts[1:]:
        level = level * one(*cut)
    return level


def scatter_about(stream_key, extent, width, most, shards=(), kind=jnp.bfloat16):
    drawn = width * jax.random.normal(stream_key, extent, jnp.float32)
    if shards:
        drawn = drawn * levels(stream_key, extent, shards, -0.22, 0.18)
    return jnp.clip(drawn, -most, most).astype(kind)


def setup_inputs(seed: int = 0) -> dict:
    key_list = jax.random.split(jax.random.key(seed), 18)
    tokens = draw_tokens(jax.random.fold_in(key_list[17], 71), 0)
    norm1_gain = jnp.clip(1.0 + 0.18 * jax.random.normal(key_list[1], (WIDTH,), jnp.float32), 0.1, 1.9)
    w_z = scatter_about(key_list[2], (WIDTH, HEADS * HEAD_DIM), WIDTH ** -0.5, 0.125, ((1, 8),))
    w_x = scatter_about(key_list[3], (WIDTH, HEADS * HEAD_DIM), WIDTH ** -0.5, 0.125, ((1, 8),))
    w_bc = scatter_about(key_list[4], (WIDTH, 2 * STATE_DIM), WIDTH ** -0.5, 0.125)
    w_dt = draw_w_dt(jax.random.fold_in(key_list[17], 71), 0)
    dt_bias = jnp.clip(-5.5 + 1.5 * jax.random.uniform(key_list[6], (HEADS,), jnp.float32) ** levels(key_list[6], (HEADS,), ((0, 8),), -0.2, 0.2), -5.5, -4.0)
    a_log = draw_a_log(jax.random.fold_in(key_list[17], 71), 0)
    conv_x = scatter_about(key_list[8], (4, HEADS * HEAD_DIM), 4 ** -0.5, 3.0, ((1, 8),), jnp.float32)
    conv_bc = scatter_about(key_list[9], (4, 2 * STATE_DIM), 4 ** -0.5, 3.0, (), jnp.float32)
    d_skip = jnp.clip(1.0 + 0.18 * jax.random.normal(key_list[10], (HEADS,), jnp.float32), 0.1, 1.9)
    ssm_gain = jnp.clip(1.0 + 0.18 * jax.random.normal(key_list[11], (HEADS * HEAD_DIM,), jnp.float32), 0.1, 1.9)
    w_out = scatter_about(key_list[12], (HEADS * HEAD_DIM, WIDTH), (HEADS * HEAD_DIM) ** -0.5, 0.078125, ((0, 8),))
    norm2_gain = jnp.clip(1.0 + 0.18 * jax.random.normal(key_list[13], (WIDTH,), jnp.float32), 0.1, 1.9)
    w_gate = scatter_about(key_list[14], (WIDTH, MLP_DIM), WIDTH ** -0.5, 0.125, ((1, 8),))
    w_up = scatter_about(key_list[15], (WIDTH, MLP_DIM), WIDTH ** -0.5, 0.125, ((1, 8),))
    w_down = scatter_about(key_list[16], (MLP_DIM, WIDTH), MLP_DIM ** -0.5, 0.078125, ((0, 8),))
    return dict(tokens=tokens, norm1_gain=norm1_gain, w_z=w_z, w_x=w_x, w_bc=w_bc, w_dt=w_dt, dt_bias=dt_bias, a_log=a_log, conv_x=conv_x, conv_bc=conv_bc, d_skip=d_skip, ssm_gain=ssm_gain, w_out=w_out, norm2_gain=norm2_gain, w_gate=w_gate, w_up=w_up, w_down=w_down)


EPS = 1e-05

def rms_rows(values, gain):
    wide = values.astype(jnp.float32)
    return wide * lax.rsqrt(lax.optimization_barrier(jnp.mean(wide * wide, axis=-1, keepdims=True)) + EPS) * gain

def conv_four(rim, current, kernel):
    extended = jnp.concatenate([rim, current], axis=0).astype(jnp.float32)
    length = current.shape[0]
    result = kernel[0] * extended[0:length]
    for offset in range(1, 4):
        result = result + kernel[offset] * extended[offset:offset + length]
    return result

def split_sum(left, right):
    groups = N_TP
    inner_len = left.shape[1] // groups
    left_parts = left.reshape(left.shape[0], groups, inner_len).astype(jnp.float32)
    right_parts = right.reshape(groups, inner_len, right.shape[1]).astype(jnp.float32)
    partial_sums = jnp.einsum('tkc,kcd->ktd', left_parts, right_parts).astype(jnp.bfloat16)
    partial_sums = lax.optimization_barrier(partial_sums)
    return lax.optimization_barrier(jnp.sum(partial_sums.astype(jnp.float32), axis=0))

def reference(tokens, norm1_gain, w_z, w_x, w_bc, w_dt, dt_bias, a_log, conv_x, conv_bc, d_skip, ssm_gain, w_out, norm2_gain, w_gate, w_up, w_down):
    block_count = SEQ_LEN // BLOCK_LEN
    channels = HEADS * HEAD_DIM
    causal_mask = jnp.tril(jnp.ones((BLOCK_LEN, BLOCK_LEN), dtype=bool))

    def block_step(carry, block_tokens):
        state, rim_inner, rim_bc = carry
        normed = rms_rows(block_tokens, norm1_gain).astype(jnp.bfloat16)
        gate_z = jnp.dot(normed, w_z, preferred_element_type=jnp.float32)
        inner_rows = jnp.dot(normed, w_x, preferred_element_type=jnp.float32).astype(jnp.bfloat16)
        bc_rows = jnp.dot(normed, w_bc, preferred_element_type=jnp.float32).astype(jnp.bfloat16)
        dt_raw = jnp.dot(normed, w_dt, preferred_element_type=jnp.float32)
        conv_inner = jax.nn.silu(conv_four(rim_inner, inner_rows, conv_x)).astype(jnp.bfloat16)
        conv_bcm = jax.nn.silu(conv_four(rim_bc, bc_rows, conv_bc)).astype(jnp.bfloat16)
        dt_step = jax.nn.softplus(dt_raw + dt_bias)
        log_decay = -dt_step * jnp.exp(a_log)
        cum_decay = jnp.cumsum(log_decay, axis=0)
        b_mat = conv_bcm[:, :STATE_DIM]
        c_mat = conv_bcm[:, STATE_DIM:]
        scores = jnp.dot(c_mat, b_mat.T, preferred_element_type=jnp.float32)
        decay_diff = jnp.where(causal_mask[:, :, None], cum_decay[:, None, :] - cum_decay[None, :, :], 0.0)
        weights = jnp.where(causal_mask[:, :, None], jnp.exp(decay_diff), 0.0)
        inner_wide = conv_inner.astype(jnp.float32).reshape(BLOCK_LEN, HEADS, HEAD_DIM)
        scaled = inner_wide * dt_step[:, :, None]
        mixed_w = scores[:, :, None] * weights
        y_intra = jnp.einsum('tsh,shp->thp', mixed_w, scaled, precision=lax.Precision.HIGHEST)
        c_wide = c_mat.astype(jnp.float32)
        b_wide = b_mat.astype(jnp.float32)
        y_inter = jnp.exp(cum_decay)[:, :, None] * jnp.einsum('tn,hpn->thp', c_wide, state, precision=lax.Precision.HIGHEST)
        ssm_out = y_intra + y_inter + d_skip[None, :, None] * inner_wide
        block_last = cum_decay[-1]
        tail_decay = jnp.exp(block_last[None, :] - cum_decay)
        fresh = jnp.einsum('sh,shp,sn->hpn', tail_decay, scaled, b_wide, precision=lax.Precision.HIGHEST)
        new_state = jnp.exp(block_last)[:, None, None] * state + fresh
        gated = ssm_out.reshape(BLOCK_LEN, channels) * jax.nn.silu(gate_z)
        scaled_out = (gated * lax.rsqrt(lax.optimization_barrier(jnp.mean(gated * gated, axis=-1, keepdims=True)) + EPS) * ssm_gain).astype(jnp.bfloat16)
        mixer = split_sum(scaled_out, w_out)
        resid = (block_tokens.astype(jnp.float32) + mixer).astype(jnp.bfloat16)
        mlp_in = rms_rows(resid, norm2_gain).astype(jnp.bfloat16)
        mlp_gate = jnp.dot(mlp_in, w_gate, preferred_element_type=jnp.float32)
        mlp_up = jnp.dot(mlp_in, w_up, preferred_element_type=jnp.float32)
        hidden = (jax.nn.silu(mlp_gate) * mlp_up).astype(jnp.bfloat16)
        mlp_down = split_sum(hidden, w_down)
        layer_out = (resid.astype(jnp.float32) + mlp_down).astype(jnp.bfloat16)
        return ((new_state, inner_rows[-3:], bc_rows[-3:]), layer_out)
    start_state = jnp.zeros((HEADS, HEAD_DIM, STATE_DIM), jnp.float32)
    start_inner = jnp.zeros((3, channels), jnp.bfloat16)
    start_bc = jnp.zeros((3, 2 * STATE_DIM), jnp.bfloat16)
    blocks = tokens.reshape(block_count, BLOCK_LEN, WIDTH)
    final_carry, outputs = lax.scan(block_step, (start_state, start_inner, start_bc), blocks)
    return outputs.reshape(SEQ_LEN, WIDTH)
```

```python
import functools

import jax
import jax.numpy as jnp
from jax import lax
from jax.experimental import pallas as pl
from jax.experimental.pallas import tpu as pltpu
from jax.sharding import PartitionSpec as P

HEADS = 80
HEAD_DIM = 64
STATE_DIM = 128
BLOCK_LEN = 256
EPS = 1e-05
F32 = jnp.float32
BF16 = jnp.bfloat16
MESH = pl.DeviceIdType.MESH
VMEM_LIMIT = 60 * 1024 * 1024


def from_behind(value, axis, steps):
    count = lax.axis_size(axis)
    first, last = (max(0, -steps), min(count, count - steps))
    return lax.ppermute(value, axis, [(source, source + steps) for source in range(first, last)])


def rms_rows(values, gain):
    wide = values.astype(F32)
    return wide * lax.rsqrt(jnp.mean(wide * wide, axis=-1, keepdims=True) + EPS) * gain


def conv_four(rim, current, kernel):
    extended = jnp.concatenate([rim, current], axis=0).astype(F32)
    length = current.shape[0]
    result = kernel[0] * extended[0:length]
    for offset in range(1, 4):
        result = result + kernel[offset] * extended[offset : offset + length]
    return result


def silu(x):
    return x / (1.0 + jnp.exp(-x))


def place():
    me = lax.axis_index("tp")
    return me, me // 2, me % 2


def greet(peers, number):
    barrier = pltpu.get_barrier_semaphore()
    for cond, peer in peers:

        @pl.when(cond)
        def _():
            pl.semaphore_signal(barrier, inc=1, device_id={"tp": peer}, device_id_type=MESH)

    pl.semaphore_wait(barrier, number)


def remote(src, dst, send, recv, peer):
    return pltpu.make_async_remote_copy(
        src_ref=src, dst_ref=dst, send_sem=send, recv_sem=recv,
        device_id={"tp": peer}, device_id_type=MESH,
    )


class Gather:
    def __init__(self, held, sems, chips, rows):
        self.held, self.sems, self.chips, self.rows = held, sems, chips, rows
        self.me, self.z, self.c = place()

    def half(self, chip, core):
        return self.held.at[chip, pl.ds(pl.multiple_of(core * self.rows, 16), self.rows)]

    def copy(self, kind, chip, core):
        send, recv = self.sems
        peer = (self.me + 2, self.me - 2, self.z * 2 + 1 - self.c)[kind]
        part = self.half(chip, core)
        return remote(part, part, send.at[kind, chip], recv.at[kind, chip], peer)

    def start(self):
        @pl.when(self.z < self.chips - 1)
        def _():
            self.copy(0, self.z, self.c).start()

        @pl.when(self.z > 0)
        def _():
            self.copy(1, self.z, self.c).start()

        self.copy(2, self.z, self.c).start()

    def arrive(self, step):
        below, above = self.z - 1 - step, self.z + 1 + step

        @pl.when(below >= 0)
        def _():
            self.copy(0, below, self.c).wait_recv()

            @pl.when(self.z < self.chips - 1)
            def _():
                self.copy(0, below, self.c).start()

            self.copy(2, below, self.c).start()

        @pl.when(above < self.chips)
        def _():
            self.copy(1, above, self.c).wait_recv()

            @pl.when(self.z > 0)
            def _():
                self.copy(1, above, self.c).start()

            self.copy(2, above, self.c).start()

    def both(self, chip):
        self.copy(2, chip, 1 - self.c).wait_recv()

    def finish(self):
        @pl.loop(0, self.chips)
        def _(chip):
            @pl.when((chip <= self.z) & (self.z < self.chips - 1))
            def _():
                self.copy(0, chip, self.c).wait_send()

            @pl.when((chip >= self.z) & (self.z > 0))
            def _():
                self.copy(1, chip, self.c).wait_send()

            self.copy(2, chip, self.c).wait_send()


def project_kernel(
    chips, rows, tok, gain, w_z, w_x, w_bc, w_dt, z_out, x_out, bc_out, dt_out, held, send, recv
):
    me, z, c = place()
    greet(
        [(z < chips - 1, me + 2), (z > 0, me - 2), (z >= 0, z * 2 + 1 - c)],
        1 + (z < chips - 1).astype(jnp.int32) + (z > 0).astype(jnp.int32),
    )
    gather = Gather(held, (send, recv), chips, rows)
    held[z, pl.ds(pl.multiple_of(c * rows, 16), rows)] = rms_rows(tok[...], gain[...]).astype(BF16)
    gather.start()

    def work(chip):
        gather.both(chip)
        here = pl.ds(pl.multiple_of(chip * 2 * rows, 16), 2 * rows)
        bc_out[here] = jnp.dot(held[chip], w_bc[...], preferred_element_type=F32).astype(BF16)
        dt_out[here] = jnp.dot(held[chip], w_dt[...], preferred_element_type=F32)
        x_out[here] = jnp.dot(held[chip], w_x[...], preferred_element_type=F32).astype(BF16)
        z_out[here] = jnp.dot(held[chip], w_z[...], preferred_element_type=F32)

    work(z)

    @pl.loop(0, chips - 1)
    def _(step):
        gather.arrive(step)

        @pl.loop(0, 2)
        def _(side):
            chip = z + (1 + step) * (2 * side - 1)

            @pl.when((chip >= 0) & (chip < chips))
            def _():
                work(chip)

    gather.finish()


def project(tokens, gain, w_z, w_x, w_bc, w_dt, chips):
    rows = tokens.shape[0]
    total = rows * chips * 2
    spec = pl.BlockSpec(memory_space=pltpu.VMEM)
    return pl.pallas_call(
        functools.partial(project_kernel, chips, rows),
        out_shape=(
            jax.ShapeDtypeStruct((total, w_z.shape[1]), F32),
            jax.ShapeDtypeStruct((total, w_x.shape[1]), BF16),
            jax.ShapeDtypeStruct((total, w_bc.shape[1]), BF16),
            jax.ShapeDtypeStruct((total, w_dt.shape[1]), F32),
        ),
        in_specs=[spec] * 6,
        out_specs=(spec,) * 4,
        scratch_shapes=[
            pltpu.VMEM((chips, 2 * rows, tokens.shape[1]), BF16),
            pltpu.SemaphoreType.DMA((3, chips)),
            pltpu.SemaphoreType.DMA((3, chips)),
        ],
        compiler_params=pltpu.CompilerParams(
            collective_id=0, has_side_effects=True, vmem_limit_bytes=VMEM_LIMIT
        ),
        name="project",
    )(tokens, gain, w_z, w_x, w_bc, w_dt)


def scan_kernel(heads, x_ref, bc_ref, z_ref, dt_ref, dtr_ref, cum_ref, cumr_ref, skip_ref, gain_ref,
                start_ref, out_ref, sq_ref, state, scaled, gated):
    @pl.when(pl.program_id(0) == 0)
    def _():
        state[...] = start_ref[...]

    length = x_ref.shape[0]
    b_mat = bc_ref[:, :STATE_DIM]
    c_mat = bc_ref[:, STATE_DIM:]
    contract_last = (((1,), (1,)), ((), ()))
    scores = lax.dot_general(c_mat, b_mat, contract_last, preferred_element_type=F32)
    carried = lax.dot_general(c_mat, state[...].astype(BF16), contract_last, preferred_element_type=F32)
    row = lax.broadcasted_iota(jnp.int32, (length, length), 0)
    col = lax.broadcasted_iota(jnp.int32, (length, length), 1)
    causal = row >= col
    for h in range(heads):
        lanes = slice(h * HEAD_DIM, (h + 1) * HEAD_DIM)
        cum = cum_ref[:, h : h + 1]
        cum_row = cumr_ref[h : h + 1, :]
        last = cumr_ref[h : h + 1, length - 1 : length]
        weight = jnp.exp(jnp.where(causal, cum - cum_row, -1e30))
        mixed = (scores * weight * dtr_ref[h : h + 1, :]).astype(BF16)
        x_head = x_ref[:, lanes]
        x_wide = x_head.astype(F32)
        y = jnp.dot(mixed, x_head, preferred_element_type=F32)
        y = y + jnp.exp(cum) * carried[:, lanes] + skip_ref[:, lanes] * x_wide
        gated[:, lanes] = y * silu(z_ref[:, lanes])
        scaled[:, lanes] = (x_wide * (jnp.exp(last - cum) * dt_ref[:, h : h + 1])).astype(BF16)
        state[lanes, :] = state[lanes, :] * jnp.exp(last)
    state[...] += lax.dot_general(
        scaled[...], b_mat, (((0,), (0,)), ((), ())), preferred_element_type=F32
    )
    g = gated[...]
    out_ref[...] = (g * gain_ref[...]).astype(BF16)
    sq_ref[...] = lax.dot_general(
        jnp.ones((8, g.shape[1]), F32), g * g, contract_last,
        preferred_element_type=F32, precision=lax.Precision.HIGHEST,
    )


def scan(x, bc, z, dt, cum, skip, gain, start):
    total, channels = x.shape
    heads = dt.shape[1]
    by_row = lambda width: pl.BlockSpec((BLOCK_LEN, width), lambda i: (i, 0))
    by_col = lambda height: pl.BlockSpec((height, BLOCK_LEN), lambda i: (0, i))
    whole = lambda shape: pl.BlockSpec(shape, lambda i: (0, 0))
    return pl.pallas_call(
        functools.partial(scan_kernel, heads),
        grid=(total // BLOCK_LEN,),
        out_shape=(
            jax.ShapeDtypeStruct((total, channels), BF16),
            jax.ShapeDtypeStruct((8, total), F32),
        ),
        in_specs=[
            by_row(channels), by_row(bc.shape[1]), by_row(channels), by_row(heads), by_col(heads),
            by_row(heads), by_col(heads), whole((1, channels)), whole((1, channels)),
            whole((channels, STATE_DIM)),
        ],
        out_specs=(by_row(channels), by_col(8)),
        scratch_shapes=[
            pltpu.VMEM((channels, STATE_DIM), F32),
            pltpu.VMEM((BLOCK_LEN, channels), BF16),
            pltpu.VMEM((BLOCK_LEN, channels), F32),
        ],
        compiler_params=pltpu.CompilerParams(vmem_limit_bytes=VMEM_LIMIT),
        name="scan",
    )(x, bc, z, dt, dt.T, cum, cum.T, skip, gain, start)


PIECES = 4


def layer_kernel(
    chips, rows, g_ref, sq_ref, tok, gain, w_out, w_gate, w_up, w_down, out,
    part, sib, chain, held, part2, sib2, chain2, squares, resid, hidden,
    sq_send, sq_recv, sib_send, sib_recv, ch_send, ch_recv, ag_send, ag_recv,
    sib2_send, sib2_recv, ch2_send, ch2_recv,
):
    me, z, c = place()
    count = 2 * chips
    width = tok.shape[1]
    tile = width // PIECES
    other = z * 2 + 1 - c
    greet([(me != peer, jnp.int32(peer)) for peer in range(count)], count - 1)

    def sq_copy(src, slot, peer):
        return remote(sq_ref.at[src], squares.at[slot], sq_send.at[src], sq_recv.at[slot], peer)

    @pl.loop(0, count)
    def _(peer):
        @pl.when(peer != me)
        def _():
            sq_copy(peer, me, peer).start()

    def mine(ref, chip, core):
        return ref.at[chip, pl.ds(pl.multiple_of(core * rows, 16), rows)]

    def own_rows():
        return pl.ds(pl.multiple_of(c * rows, 16), rows)

    def swap(chip):
        return remote(mine(part, chip, 1 - c), sib.at[chip], sib_send.at[chip], sib_recv.at[chip], other)

    def product(chip):
        here = pl.ds(pl.multiple_of(chip * 2 * rows, 16), 2 * rows)

        @pl.loop(0, PIECES)
        def _(k):
            cols = pl.ds(pl.multiple_of(k * tile, 128), tile)
            part[chip, :, cols] = jnp.dot(
                g_ref[here], w_out[:, cols], preferred_element_type=F32
            ).astype(BF16)

        swap(chip).start()

    def move(way, chip, step):
        peer = me + 2 - 4 * way
        return remote(mine(part, chip, c), chain.at[way, step], ch_send.at[way, step], ch_recv.at[way, step], peer)

    def add(chip, way, step, use_chain):
        @pl.loop(0, PIECES)
        def _(k):
            cols = pl.ds(pl.multiple_of(k * tile, 128), tile)
            value = part[chip, own_rows(), cols].astype(F32)
            if use_chain:
                value = value + chain[way, step, :, cols].astype(F32)
            else:
                value = value + sib[chip, :, cols].astype(F32)
            part[chip, own_rows(), cols] = value.astype(BF16)

    def ends(way):
        return (z, z < chips - 1) if way == 0 else (chips - 1 - z, z > 0)

    def target(way, step):
        return chips - 1 + z - step if way == 0 else step + z - (chips - 1)

    @pl.loop(0, chips - 1)
    def _(step):
        for way in (0, 1):
            behind, more = ends(way)

            @pl.when((behind <= step) & more)
            def _():
                product(target(way, step))

        for way in (0, 1):
            behind, more = ends(way)
            chip = target(way, step)

            @pl.when((behind <= step) & more)
            def _():
                swap(chip).wait_recv()
                add(chip, way, step, False)

                @pl.when(behind > 0)
                def _():
                    move(way, chip, step - 1).wait_recv()
                    add(chip, way, step - 1, True)

                move(way, chip, step).start()

    product(z)

    @pl.loop(0, count)
    def _(peer):
        @pl.when(peer != me)
        def _():
            sq_copy(peer, peer, peer).wait_recv()

    squares[me] = sq_ref[me]
    total_sq = squares[0]
    for peer in range(1, count):
        total_sq = total_sq + squares[peer]
    row = lax.broadcasted_iota(jnp.int32, (rows, rows), 0)
    col = lax.broadcasted_iota(jnp.int32, (rows, rows), 1)
    as_column = jnp.sum(jnp.where(row == col, total_sq[0:1], 0.0), axis=1, keepdims=True)
    scale = lax.rsqrt(as_column / (HEADS * HEAD_DIM) + EPS)

    swap(z).wait_recv()
    add(z, 0, 0, False)
    for way in (0, 1):
        behind, more = ends(way)

        @pl.when(behind > 0)
        def _():
            move(way, z, chips - 2).wait_recv()
            add(z, way, chips - 2, True)

    value = (tok[...].astype(F32) + part[z, own_rows()].astype(F32) * scale).astype(BF16)
    resid[...] = value
    held[z, own_rows()] = rms_rows(value, gain[...]).astype(BF16)

    gather = Gather(held, (ag_send, ag_recv), chips, rows)
    gather.start()

    def swap2(chip):
        return remote(mine(part2, chip, 1 - c), sib2.at[chip], sib2_send.at[chip], sib2_recv.at[chip], other)

    def mlp(chip):
        gather.both(chip)
        gate = jnp.dot(held[chip], w_gate[...], preferred_element_type=F32)
        up = jnp.dot(held[chip], w_up[...], preferred_element_type=F32)
        hidden[...] = (silu(gate) * up).astype(BF16)

        @pl.loop(0, PIECES)
        def _(k):
            cols = pl.ds(pl.multiple_of(k * tile, 128), tile)
            part2[chip, :, cols] = jnp.dot(
                hidden[...], w_down[:, cols], preferred_element_type=F32
            ).astype(BF16)

        swap2(chip).start()

    def move2(way, chip, k):
        peer = me + 2 - 4 * way
        cols = pl.ds(pl.multiple_of(k * tile, 128), tile)
        return remote(
            part2.at[chip, own_rows(), cols], chain2.at[way, chip, :, cols],
            ch2_send.at[way, chip, k], ch2_recv.at[way, chip, k], peer,
        )

    def pass_on(step):
        for way in (0, 1):
            behind, more = ends(way)
            chip = step + 1 if way == 0 else chips - 2 - step
            before = (z < chip) if way == 0 else (z > chip)

            @pl.when(before)
            def _():
                swap2(chip).wait_recv()

                @pl.loop(0, PIECES)
                def _(k):
                    cols = pl.ds(pl.multiple_of(k * tile, 128), tile)
                    part2[chip, own_rows(), cols] = (
                        part2[chip, own_rows(), cols].astype(F32) + sib2[chip, :, cols].astype(F32)
                    ).astype(BF16)

                    @pl.when(behind > 0)
                    def _():
                        move2(way, chip, k).wait_recv()
                        part2[chip, own_rows(), cols] = (
                            part2[chip, own_rows(), cols].astype(F32)
                            + chain2[way, chip, :, cols].astype(F32)
                        ).astype(BF16)

                    move2(way, chip, k).start()

    mlp(z)

    @pl.loop(0, chips - 1)
    def _(step):
        gather.arrive(step)

        @pl.loop(0, 2)
        def _(side):
            chip = z + (1 + step) * (2 * side - 1)

            @pl.when((chip >= 0) & (chip < chips))
            def _():
                mlp(chip)

        @pl.when(step > 0)
        def _():
            pass_on(step - 1)

    pass_on(chips - 2)

    swap2(z).wait_recv()

    @pl.loop(0, PIECES)
    def _(k):
        cols = pl.ds(pl.multiple_of(k * tile, 128), tile)
        part2[z, own_rows(), cols] = (
            part2[z, own_rows(), cols].astype(F32) + sib2[z, :, cols].astype(F32)
        ).astype(BF16)
        for way in (0, 1):
            behind, more = ends(way)

            @pl.when(behind > 0)
            def _():
                move2(way, z, k).wait_recv()
                part2[z, own_rows(), cols] = (
                    part2[z, own_rows(), cols].astype(F32) + chain2[way, z, :, cols].astype(F32)
                ).astype(BF16)

        out[:, cols] = (
            resid[:, cols].astype(F32) + part2[z, own_rows(), cols].astype(F32)
        ).astype(BF16)

    gather.finish()

    @pl.loop(0, count)
    def _(peer):
        @pl.when(peer != me)
        def _():
            sq_copy(peer, me, peer).wait_send()

    @pl.loop(0, chips)
    def _(chip):
        swap(chip).wait_send()
        swap2(chip).wait_send()

    @pl.loop(0, chips - 1)
    def _(step):
        for way in (0, 1):
            behind, more = ends(way)
            chip = step + 1 if way == 0 else chips - 2 - step
            before = (z < chip) if way == 0 else (z > chip)

            @pl.when((behind <= step) & more)
            def _():
                move(way, target(way, step), step).wait_send()

            @pl.when(before)
            def _():
                @pl.loop(0, PIECES)
                def _(k):
                    move2(way, chip, k).wait_send()


def layer(g, sq, tokens, gain, w_out, w_gate, w_up, w_down, chips):
    rows, width = tokens.shape
    spec = pl.BlockSpec(memory_space=pltpu.VMEM)
    dma = pltpu.SemaphoreType.DMA
    return pl.pallas_call(
        functools.partial(layer_kernel, chips, rows),
        out_shape=jax.ShapeDtypeStruct((rows, width), BF16),
        in_specs=[spec] * 8,
        out_specs=spec,
        scratch_shapes=[
            pltpu.VMEM((chips, 2 * rows, width), BF16),
            pltpu.VMEM((chips, rows, width), BF16),
            pltpu.VMEM((2, chips - 1, rows, width), BF16),
            pltpu.VMEM((chips, 2 * rows, width), BF16),
            pltpu.VMEM((chips, 2 * rows, width), BF16),
            pltpu.VMEM((chips, rows, width), BF16),
            pltpu.VMEM((2, chips, rows, width), BF16),
            pltpu.VMEM((2 * chips, 8, rows), F32),
            pltpu.VMEM((rows, width), BF16),
            pltpu.VMEM((2 * rows, w_gate.shape[1]), BF16),
            dma((2 * chips,)), dma((2 * chips,)),
            dma((chips,)), dma((chips,)),
            dma((2, chips - 1)), dma((2, chips - 1)),
            dma((3, chips)), dma((3, chips)),
            dma((chips,)), dma((chips,)),
            dma((2, chips, PIECES)), dma((2, chips, PIECES)),
        ],
        compiler_params=pltpu.CompilerParams(
            collective_id=1, has_side_effects=True, vmem_limit_bytes=VMEM_LIMIT
        ),
        name="mixer_out_and_mlp",
    )(g, sq, tokens, gain, w_out, w_gate, w_up, w_down)


def local(
    tokens, norm1_gain, w_z, w_x, w_bc, w_dt, dt_bias, a_log, conv_x, conv_bc, d_skip, ssm_gain,
    w_out, norm2_gain, w_gate, w_up, w_down,
):
    count = lax.axis_size("tp")
    chips = count // 2
    rows = tokens.shape[0]
    heads = w_dt.shape[1]
    gate_z, inner_rows, bc_rows, dt_raw = project(
        tokens, norm1_gain[None], w_z, w_x, w_bc, w_dt, chips
    )
    group_len = inner_rows.shape[0]
    blocks = group_len // BLOCK_LEN
    rim = from_behind(jnp.concatenate([inner_rows[-3:], bc_rows[-3:]], axis=1), "ctx", 1)
    rim_inner, rim_bc = rim[:, : inner_rows.shape[1]], rim[:, inner_rows.shape[1] :]
    conv_inner = jax.nn.silu(conv_four(rim_inner, inner_rows, conv_x)).astype(BF16)
    conv_bcm = jax.nn.silu(conv_four(rim_bc, bc_rows, conv_bc)).astype(BF16)
    dt_step = jax.nn.softplus(dt_raw + dt_bias)
    log_decay = -dt_step * jnp.exp(a_log)
    cum = jnp.cumsum(log_decay.reshape(blocks, BLOCK_LEN, heads), axis=1)
    block_last = cum[:, -1, :]
    later = jnp.cumsum(block_last[::-1], axis=0)[::-1] - block_last
    tail = jnp.exp((block_last + later)[:, None] - cum) * dt_step.reshape(cum.shape)
    spread = jnp.repeat(jnp.eye(heads, dtype=F32), HEAD_DIM, axis=1)
    tail_wide = jnp.dot(tail.reshape(group_len, heads), spread, precision=lax.Precision.HIGHEST)
    final = lax.dot_general(
        (conv_inner.astype(F32) * tail_wide).astype(BF16),
        conv_bcm[:, :STATE_DIM],
        (((0,), (0,)), ((), ())),
        preferred_element_type=F32,
    )
    total_decay = jnp.exp(jnp.sum(block_last, axis=0))
    carried = jnp.concatenate(
        [final, jnp.broadcast_to(total_decay[:, None], (heads, STATE_DIM))], axis=0
    ).astype(BF16)
    gathered = lax.all_gather(carried, "ctx").astype(F32)
    channels = final.shape[0]
    start = jnp.zeros((heads, HEAD_DIM, STATE_DIM), F32)
    for step in range(lax.axis_size("ctx") - 1):
        fresh = gathered[step, :channels].reshape(start.shape)
        after = gathered[step, channels:][:, None, :] * start + fresh
        start = jnp.where(step < lax.axis_index("ctx"), after, start)
    gated, squares = scan(
        conv_inner, conv_bcm, gate_z, dt_step, cum.reshape(group_len, heads),
        jnp.repeat(d_skip, HEAD_DIM)[None], ssm_gain[None], start.reshape(channels, STATE_DIM),
    )
    squares = squares.reshape(8, count, rows).transpose(1, 0, 2)
    return layer(gated, squares, tokens, norm2_gain[None], w_out, w_gate, w_up, w_down, chips)


def solution(mesh):
    return jax.shard_map(
        local,
        mesh=mesh,
        in_specs=(
            P(("ctx", "tp"), None),
            P(),
            P(None, "tp"),
            P(None, "tp"),
            P(),
            P(None, "tp"),
            P("tp"),
            P("tp"),
            P(None, "tp"),
            P(),
            P("tp"),
            P("tp"),
            P("tp", None),
            P(),
            P(None, "tp"),
            P(None, "tp"),
            P("tp", None),
        ),
        out_specs=P(("ctx", "tp"), None),
        check_vma=False,
    )
```

```python
import functools

import jax
import jax.numpy as jnp
from jax import lax
from jax.experimental import pallas as pl
from jax.experimental.pallas import tpu as pltpu
from jax.sharding import PartitionSpec as P

HEADS = 80
HEAD_DIM = 64
STATE_DIM = 128
BLOCK_LEN = 256
EPS = 1e-05
F32 = jnp.float32
BF16 = jnp.bfloat16
MESH = pl.DeviceIdType.MESH
VMEM_LIMIT = 60 * 1024 * 1024


def from_behind(value, axis, steps):
    count = lax.axis_size(axis)
    first, last = (max(0, -steps), min(count, count - steps))
    return lax.ppermute(value, axis, [(source, source + steps) for source in range(first, last)])


def rms_rows(values, gain):
    wide = values.astype(F32)
    return wide * lax.rsqrt(jnp.mean(wide * wide, axis=-1, keepdims=True) + EPS) * gain


def conv_four(rim, current, kernel):
    extended = jnp.concatenate([rim, current], axis=0).astype(F32)
    length = current.shape[0]
    result = kernel[0] * extended[0:length]
    for offset in range(1, 4):
        result = result + kernel[offset] * extended[offset : offset + length]
    return result


def silu(x):
    return x / (1.0 + jnp.exp(-x))


def place():
    me = lax.axis_index("tp")
    return me, me // 2, me % 2


def greet(peers, number):
    barrier = pltpu.get_barrier_semaphore()
    for cond, peer in peers:

        @pl.when(cond)
        def _():
            pl.semaphore_signal(barrier, inc=1, device_id={"tp": peer}, device_id_type=MESH)

    pl.semaphore_wait(barrier, number)


def remote(src, dst, send, recv, peer):
    return pltpu.make_async_remote_copy(
        src_ref=src, dst_ref=dst, send_sem=send, recv_sem=recv,
        device_id={"tp": peer}, device_id_type=MESH,
    )


class Gather:
    def __init__(self, held, sems, chips, rows, part=0, parts=1):
        self.held, self.sems, self.chips, self.rows = held, sems, chips, rows
        self.size = rows // parts
        self.part = part
        self.me, self.z, self.c = place()

    def half(self, chip, core):
        first = pl.multiple_of(core * self.rows + self.part * self.size, 16)
        return self.held.at[chip, pl.ds(first, self.size)]

    def copy(self, kind, chip, core):
        send, recv = self.sems
        peer = (self.me + 2, self.me - 2, self.z * 2 + 1 - self.c)[kind]
        part = self.half(chip, core)
        slot = self.part * 3 + kind
        return remote(part, part, send.at[slot, chip], recv.at[slot, chip], peer)

    def start(self):
        @pl.when(self.z < self.chips - 1)
        def _():
            self.copy(0, self.z, self.c).start()

        @pl.when(self.z > 0)
        def _():
            self.copy(1, self.z, self.c).start()

        self.copy(2, self.z, self.c).start()

    def arrive(self, step):
        below, above = self.z - 1 - step, self.z + 1 + step

        @pl.when(below >= 0)
        def _():
            self.copy(0, below, self.c).wait_recv()

            @pl.when(self.z < self.chips - 1)
            def _():
                self.copy(0, below, self.c).start()

            self.copy(2, below, self.c).start()

        @pl.when(above < self.chips)
        def _():
            self.copy(1, above, self.c).wait_recv()

            @pl.when(self.z > 0)
            def _():
                self.copy(1, above, self.c).start()

            self.copy(2, above, self.c).start()

    def both(self, chip):
        self.copy(2, chip, 1 - self.c).wait_recv()

    def finish(self):
        @pl.loop(0, self.chips)
        def _(chip):
            @pl.when((chip <= self.z) & (self.z < self.chips - 1))
            def _():
                self.copy(0, chip, self.c).wait_send()

            @pl.when((chip >= self.z) & (self.z > 0))
            def _():
                self.copy(1, chip, self.c).wait_send()

            self.copy(2, chip, self.c).wait_send()


def project_kernel(
    chips, rows, tok, gain, w_z, w_x, w_bc, w_dt, z_out, x_out, bc_out, dt_out, held, send, recv
):
    me, z, c = place()
    greet(
        [(z < chips - 1, me + 2), (z > 0, me - 2), (z >= 0, z * 2 + 1 - c)],
        1 + (z < chips - 1).astype(jnp.int32) + (z > 0).astype(jnp.int32),
    )
    gather = Gather(held, (send, recv), chips, rows)
    held[z, pl.ds(pl.multiple_of(c * rows, 16), rows)] = rms_rows(tok[...], gain[...]).astype(BF16)
    gather.start()

    def work(chip):
        gather.both(chip)
        here = pl.ds(pl.multiple_of(chip * 2 * rows, 16), 2 * rows)
        bc_out[here] = jnp.dot(held[chip], w_bc[...], preferred_element_type=F32).astype(BF16)
        dt_out[here] = jnp.dot(held[chip], w_dt[...], preferred_element_type=F32)
        x_out[here] = jnp.dot(held[chip], w_x[...], preferred_element_type=F32).astype(BF16)
        z_out[here] = jnp.dot(held[chip], w_z[...], preferred_element_type=F32)

    work(z)

    @pl.loop(0, chips - 1)
    def _(step):
        gather.arrive(step)

        @pl.loop(0, 2)
        def _(side):
            chip = z + (1 + step) * (2 * side - 1)

            @pl.when((chip >= 0) & (chip < chips))
            def _():
                work(chip)

    gather.finish()


def project(tokens, gain, w_z, w_x, w_bc, w_dt, chips):
    rows = tokens.shape[0]
    total = rows * chips * 2
    spec = pl.BlockSpec(memory_space=pltpu.VMEM)
    return pl.pallas_call(
        functools.partial(project_kernel, chips, rows),
        out_shape=(
            jax.ShapeDtypeStruct((total, w_z.shape[1]), F32),
            jax.ShapeDtypeStruct((total, w_x.shape[1]), BF16),
            jax.ShapeDtypeStruct((total, w_bc.shape[1]), BF16),
            jax.ShapeDtypeStruct((total, w_dt.shape[1]), F32),
        ),
        in_specs=[spec] * 6,
        out_specs=(spec,) * 4,
        scratch_shapes=[
            pltpu.VMEM((chips, 2 * rows, tokens.shape[1]), BF16),
            pltpu.SemaphoreType.DMA((3, chips)),
            pltpu.SemaphoreType.DMA((3, chips)),
        ],
        compiler_params=pltpu.CompilerParams(
            collective_id=0, has_side_effects=True, vmem_limit_bytes=VMEM_LIMIT
        ),
        name="project",
    )(tokens, gain, w_z, w_x, w_bc, w_dt)


def scan_kernel(heads, x_ref, bc_ref, z_ref, dt_ref, dtr_ref, cum_ref, cumr_ref, skip_ref, gain_ref,
                start_ref, out_ref, sq_ref, state, scaled, gated):
    @pl.when(pl.program_id(0) == 0)
    def _():
        state[...] = start_ref[...]

    length = x_ref.shape[0]
    b_mat = bc_ref[:, :STATE_DIM]
    c_mat = bc_ref[:, STATE_DIM:]
    contract_last = (((1,), (1,)), ((), ()))
    scores = lax.dot_general(c_mat, b_mat, contract_last, preferred_element_type=F32)
    carried = lax.dot_general(c_mat, state[...].astype(BF16), contract_last, preferred_element_type=F32)
    row = lax.broadcasted_iota(jnp.int32, (length, length), 0)
    col = lax.broadcasted_iota(jnp.int32, (length, length), 1)
    causal = row >= col
    for h in range(heads):
        lanes = slice(h * HEAD_DIM, (h + 1) * HEAD_DIM)
        cum = cum_ref[:, h : h + 1]
        cum_row = cumr_ref[h : h + 1, :]
        last = cumr_ref[h : h + 1, length - 1 : length]
        weight = jnp.exp(jnp.where(causal, cum - cum_row, -1e30))
        mixed = (scores * weight * dtr_ref[h : h + 1, :]).astype(BF16)
        x_head = x_ref[:, lanes]
        x_wide = x_head.astype(F32)
        y = jnp.dot(mixed, x_head, preferred_element_type=F32)
        y = y + jnp.exp(cum) * carried[:, lanes] + skip_ref[:, lanes] * x_wide
        gated[:, lanes] = y * silu(z_ref[:, lanes])
        scaled[:, lanes] = (x_wide * (jnp.exp(last - cum) * dt_ref[:, h : h + 1])).astype(BF16)
        state[lanes, :] = state[lanes, :] * jnp.exp(last)
    state[...] += lax.dot_general(
        scaled[...], b_mat, (((0,), (0,)), ((), ())), preferred_element_type=F32
    )
    g = gated[...]
    out_ref[...] = (g * gain_ref[...]).astype(BF16)
    sq_ref[...] = lax.dot_general(
        jnp.ones((8, g.shape[1]), F32), g * g, contract_last,
        preferred_element_type=F32, precision=lax.Precision.HIGHEST,
    )


def scan(x, bc, z, dt, cum, skip, gain, start):
    total, channels = x.shape
    heads = dt.shape[1]
    by_row = lambda width: pl.BlockSpec((BLOCK_LEN, width), lambda i: (i, 0))
    by_col = lambda height: pl.BlockSpec((height, BLOCK_LEN), lambda i: (0, i))
    whole = lambda shape: pl.BlockSpec(shape, lambda i: (0, 0))
    return pl.pallas_call(
        functools.partial(scan_kernel, heads),
        grid=(total // BLOCK_LEN,),
        out_shape=(
            jax.ShapeDtypeStruct((total, channels), BF16),
            jax.ShapeDtypeStruct((8, total), F32),
        ),
        in_specs=[
            by_row(channels), by_row(bc.shape[1]), by_row(channels), by_row(heads), by_col(heads),
            by_row(heads), by_col(heads), whole((1, channels)), whole((1, channels)),
            whole((channels, STATE_DIM)),
        ],
        out_specs=(by_row(channels), by_col(8)),
        scratch_shapes=[
            pltpu.VMEM((channels, STATE_DIM), F32),
            pltpu.VMEM((BLOCK_LEN, channels), BF16),
            pltpu.VMEM((BLOCK_LEN, channels), F32),
        ],
        compiler_params=pltpu.CompilerParams(vmem_limit_bytes=VMEM_LIMIT),
        name="scan",
    )(x, bc, z, dt, dt.T, cum, cum.T, skip, gain, start)


PIECES = 4
HALVES = 2


def layer_kernel(
    chips, rows, g_ref, sq_ref, tok, gain, w_out, w_gate, w_up, w_down, out,
    part, sib, chain, held, part2, sib2, chain2, squares, resid, hidden,
    sq_send, sq_recv, sib_send, sib_recv, ch_send, ch_recv, ag_send, ag_recv,
    sib2_send, sib2_recv, ch2_send, ch2_recv,
):
    me, z, c = place()
    count = 2 * chips
    width = tok.shape[1]
    tile = width // PIECES
    other = z * 2 + 1 - c
    greet([(me != peer, jnp.int32(peer)) for peer in range(count)], count - 1)

    def sq_copy(src, slot, peer):
        return remote(sq_ref.at[src], squares.at[slot], sq_send.at[src], sq_recv.at[slot], peer)

    @pl.loop(0, count)
    def _(peer):
        @pl.when(peer != me)
        def _():
            sq_copy(peer, me, peer).start()

    def mine(ref, chip, core):
        return ref.at[chip, pl.ds(pl.multiple_of(core * rows, 16), rows)]

    def own_rows():
        return pl.ds(pl.multiple_of(c * rows, 16), rows)

    def swap(chip):
        return remote(mine(part, chip, 1 - c), sib.at[chip], sib_send.at[chip], sib_recv.at[chip], other)

    def product(chip):
        here = pl.ds(pl.multiple_of(chip * 2 * rows, 16), 2 * rows)

        @pl.loop(0, PIECES)
        def _(k):
            cols = pl.ds(pl.multiple_of(k * tile, 128), tile)
            part[chip, :, cols] = jnp.dot(
                g_ref[here], w_out[:, cols], preferred_element_type=F32
            ).astype(BF16)

        swap(chip).start()

    size = rows // HALVES

    def some(h):
        return pl.ds(pl.multiple_of(c * rows + h * size, 16), size)

    def move(h, way, chip, step):
        peer = me + 2 - 4 * way
        slot = way * HALVES + h
        return remote(
            part.at[chip, some(h)], chain.at[way, step, pl.ds(h * size, size)],
            ch_send.at[slot, step], ch_recv.at[slot, step], peer,
        )

    def add(h, chip, way, step, use_chain):
        @pl.loop(0, PIECES)
        def _(k):
            cols = pl.ds(pl.multiple_of(k * tile, 128), tile)
            value = part[chip, some(h), cols].astype(F32)
            if use_chain:
                value = value + chain[way, step, pl.ds(h * size, size), cols].astype(F32)
            else:
                value = value + sib[chip, pl.ds(h * size, size), cols].astype(F32)
            part[chip, some(h), cols] = value.astype(BF16)

    def ends(way):
        return (z, z < chips - 1) if way == 0 else (chips - 1 - z, z > 0)

    def target(way, step):
        return chips - 1 + z - step if way == 0 else step + z - (chips - 1)

    gathers = [Gather(held, (ag_send, ag_recv), chips, rows, h, HALVES) for h in range(HALVES)]

    def forward(h, step):
        for way in (0, 1):
            behind, more = ends(way)
            chip = target(way, step)

            @pl.when((behind <= step) & more)
            def _():
                if h == 0:
                    swap(chip).wait_recv()
                add(h, chip, way, step, False)

                @pl.when(behind > 0)
                def _():
                    move(h, way, chip, step - 1).wait_recv()
                    add(h, chip, way, step - 1, True)

                move(h, way, chip, step).start()

    @pl.loop(0, chips - 1)
    def _(step):
        for way in (0, 1):
            behind, more = ends(way)

            @pl.when((behind <= step) & more)
            def _():
                product(target(way, step))

        forward(0, step)

    product(z)

    @pl.loop(0, count)
    def _(peer):
        @pl.when(peer != me)
        def _():
            sq_copy(peer, peer, peer).wait_recv()

    squares[me] = sq_ref[me]
    total_sq = squares[0]
    for peer in range(1, count):
        total_sq = total_sq + squares[peer]
    row = lax.broadcasted_iota(jnp.int32, (rows, rows), 0)
    col = lax.broadcasted_iota(jnp.int32, (rows, rows), 1)
    as_column = jnp.sum(jnp.where(row == col, total_sq[0:1], 0.0), axis=1, keepdims=True)
    scale = lax.rsqrt(as_column / (HEADS * HEAD_DIM) + EPS)

    def settle(h):
        add(h, z, 0, 0, False)
        for way in (0, 1):
            behind, more = ends(way)

            @pl.when(behind > 0)
            def _():
                move(h, way, z, chips - 2).wait_recv()
                add(h, z, way, chips - 2, True)

        here = slice(h * size, (h + 1) * size)
        value = tok[here].astype(F32) + part[z, some(h)].astype(F32) * scale[here]
        value = value.astype(BF16)
        resid[here] = value
        held[z, some(h)] = rms_rows(value, gain[...]).astype(BF16)
        gathers[h].start()

    swap(z).wait_recv()
    settle(0)
    for h in range(1, HALVES):

        @pl.loop(0, chips - 1)
        def _(step):
            forward(h, step)
            gathers[h - 1].arrive(step)

        settle(h)

    def swap2(chip):
        return remote(mine(part2, chip, 1 - c), sib2.at[chip], sib2_send.at[chip], sib2_recv.at[chip], other)

    def mlp(chip):
        for gather in gathers:
            gather.both(chip)
        gate = jnp.dot(held[chip], w_gate[...], preferred_element_type=F32)
        up = jnp.dot(held[chip], w_up[...], preferred_element_type=F32)
        hidden[...] = (silu(gate) * up).astype(BF16)

        @pl.loop(0, PIECES)
        def _(k):
            cols = pl.ds(pl.multiple_of(k * tile, 128), tile)
            part2[chip, :, cols] = jnp.dot(
                hidden[...], w_down[:, cols], preferred_element_type=F32
            ).astype(BF16)

        swap2(chip).start()

    def move2(way, chip, k):
        peer = me + 2 - 4 * way
        cols = pl.ds(pl.multiple_of(k * tile, 128), tile)
        return remote(
            part2.at[chip, own_rows(), cols], chain2.at[way, chip, :, cols],
            ch2_send.at[way, chip, k], ch2_recv.at[way, chip, k], peer,
        )

    def pass_on(step):
        for way in (0, 1):
            behind, more = ends(way)
            chip = step + 1 if way == 0 else chips - 2 - step
            before = (z < chip) if way == 0 else (z > chip)

            @pl.when(before)
            def _():
                swap2(chip).wait_recv()

                @pl.loop(0, PIECES)
                def _(k):
                    cols = pl.ds(pl.multiple_of(k * tile, 128), tile)
                    part2[chip, own_rows(), cols] = (
                        part2[chip, own_rows(), cols].astype(F32) + sib2[chip, :, cols].astype(F32)
                    ).astype(BF16)

                    @pl.when(behind > 0)
                    def _():
                        move2(way, chip, k).wait_recv()
                        part2[chip, own_rows(), cols] = (
                            part2[chip, own_rows(), cols].astype(F32)
                            + chain2[way, chip, :, cols].astype(F32)
                        ).astype(BF16)

                    move2(way, chip, k).start()

    mlp(z)

    @pl.loop(0, chips - 1)
    def _(step):
        gathers[-1].arrive(step)

        @pl.loop(0, 2)
        def _(side):
            chip = z + (1 + step) * (2 * side - 1)

            @pl.when((chip >= 0) & (chip < chips))
            def _():
                mlp(chip)

        @pl.when(step > 0)
        def _():
            pass_on(step - 1)

    pass_on(chips - 2)

    swap2(z).wait_recv()

    @pl.loop(0, PIECES)
    def _(k):
        cols = pl.ds(pl.multiple_of(k * tile, 128), tile)
        part2[z, own_rows(), cols] = (
            part2[z, own_rows(), cols].astype(F32) + sib2[z, :, cols].astype(F32)
        ).astype(BF16)
        for way in (0, 1):
            behind, more = ends(way)

            @pl.when(behind > 0)
            def _():
                move2(way, z, k).wait_recv()
                part2[z, own_rows(), cols] = (
                    part2[z, own_rows(), cols].astype(F32) + chain2[way, z, :, cols].astype(F32)
                ).astype(BF16)

        out[:, cols] = (
            resid[:, cols].astype(F32) + part2[z, own_rows(), cols].astype(F32)
        ).astype(BF16)

    for gather in gathers:
        gather.finish()

    @pl.loop(0, count)
    def _(peer):
        @pl.when(peer != me)
        def _():
            sq_copy(peer, me, peer).wait_send()

    @pl.loop(0, chips)
    def _(chip):
        swap(chip).wait_send()
        swap2(chip).wait_send()

    @pl.loop(0, chips - 1)
    def _(step):
        for way in (0, 1):
            behind, more = ends(way)
            chip = step + 1 if way == 0 else chips - 2 - step
            before = (z < chip) if way == 0 else (z > chip)

            @pl.when((behind <= step) & more)
            def _():
                for h in range(HALVES):
                    move(h, way, target(way, step), step).wait_send()

            @pl.when(before)
            def _():
                @pl.loop(0, PIECES)
                def _(k):
                    move2(way, chip, k).wait_send()


def layer(g, sq, tokens, gain, w_out, w_gate, w_up, w_down, chips):
    rows, width = tokens.shape
    spec = pl.BlockSpec(memory_space=pltpu.VMEM)
    dma = pltpu.SemaphoreType.DMA
    return pl.pallas_call(
        functools.partial(layer_kernel, chips, rows),
        out_shape=jax.ShapeDtypeStruct((rows, width), BF16),
        in_specs=[spec] * 8,
        out_specs=spec,
        scratch_shapes=[
            pltpu.VMEM((chips, 2 * rows, width), BF16),
            pltpu.VMEM((chips, rows, width), BF16),
            pltpu.VMEM((2, chips - 1, rows, width), BF16),
            pltpu.VMEM((chips, 2 * rows, width), BF16),
            pltpu.VMEM((chips, 2 * rows, width), BF16),
            pltpu.VMEM((chips, rows, width), BF16),
            pltpu.VMEM((2, chips, rows, width), BF16),
            pltpu.VMEM((2 * chips, 8, rows), F32),
            pltpu.VMEM((rows, width), BF16),
            pltpu.VMEM((2 * rows, w_gate.shape[1]), BF16),
            dma((2 * chips,)), dma((2 * chips,)),
            dma((chips,)), dma((chips,)),
            dma((2 * HALVES, chips - 1)), dma((2 * HALVES, chips - 1)),
            dma((3 * HALVES, chips)), dma((3 * HALVES, chips)),
            dma((chips,)), dma((chips,)),
            dma((2, chips, PIECES)), dma((2, chips, PIECES)),
        ],
        compiler_params=pltpu.CompilerParams(
            collective_id=1, has_side_effects=True, vmem_limit_bytes=VMEM_LIMIT
        ),
        name="mixer_out_and_mlp",
    )(g, sq, tokens, gain, w_out, w_gate, w_up, w_down)


def local(
    tokens, norm1_gain, w_z, w_x, w_bc, w_dt, dt_bias, a_log, conv_x, conv_bc, d_skip, ssm_gain,
    w_out, norm2_gain, w_gate, w_up, w_down,
):
    count = lax.axis_size("tp")
    chips = count // 2
    rows = tokens.shape[0]
    heads = w_dt.shape[1]
    gate_z, inner_rows, bc_rows, dt_raw = project(
        tokens, norm1_gain[None], w_z, w_x, w_bc, w_dt, chips
    )
    group_len = inner_rows.shape[0]
    blocks = group_len // BLOCK_LEN
    rim = from_behind(jnp.concatenate([inner_rows[-3:], bc_rows[-3:]], axis=1), "ctx", 1)
    rim_inner, rim_bc = rim[:, : inner_rows.shape[1]], rim[:, inner_rows.shape[1] :]
    conv_inner = jax.nn.silu(conv_four(rim_inner, inner_rows, conv_x)).astype(BF16)
    conv_bcm = jax.nn.silu(conv_four(rim_bc, bc_rows, conv_bc)).astype(BF16)
    dt_step = jax.nn.softplus(dt_raw + dt_bias)
    log_decay = -dt_step * jnp.exp(a_log)
    cum = jnp.cumsum(log_decay.reshape(blocks, BLOCK_LEN, heads), axis=1)
    block_last = cum[:, -1, :]
    later = jnp.cumsum(block_last[::-1], axis=0)[::-1] - block_last
    tail = jnp.exp((block_last + later)[:, None] - cum) * dt_step.reshape(cum.shape)
    spread = jnp.repeat(jnp.eye(heads, dtype=F32), HEAD_DIM, axis=1)
    tail_wide = jnp.dot(tail.reshape(group_len, heads), spread, precision=lax.Precision.HIGHEST)
    final = lax.dot_general(
        (conv_inner.astype(F32) * tail_wide).astype(BF16),
        conv_bcm[:, :STATE_DIM],
        (((0,), (0,)), ((), ())),
        preferred_element_type=F32,
    )
    total_decay = jnp.exp(jnp.sum(block_last, axis=0))
    carried = jnp.concatenate(
        [final, jnp.broadcast_to(total_decay[:, None], (heads, STATE_DIM))], axis=0
    ).astype(BF16)
    gathered = lax.all_gather(carried, "ctx").astype(F32)
    channels = final.shape[0]
    start = jnp.zeros((heads, HEAD_DIM, STATE_DIM), F32)
    for step in range(lax.axis_size("ctx") - 1):
        fresh = gathered[step, :channels].reshape(start.shape)
        after = gathered[step, channels:][:, None, :] * start + fresh
        start = jnp.where(step < lax.axis_index("ctx"), after, start)
    gated, squares = scan(
        conv_inner, conv_bcm, gate_z, dt_step, cum.reshape(group_len, heads),
        jnp.repeat(d_skip, HEAD_DIM)[None], ssm_gain[None], start.reshape(channels, STATE_DIM),
    )
    squares = squares.reshape(8, count, rows).transpose(1, 0, 2)
    return layer(gated, squares, tokens, norm2_gain[None], w_out, w_gate, w_up, w_down, chips)


def solution(mesh):
    return jax.shard_map(
        local,
        mesh=mesh,
        in_specs=(
            P(("ctx", "tp"), None),
            P(),
            P(None, "tp"),
            P(None, "tp"),
            P(),
            P(None, "tp"),
            P("tp"),
            P("tp"),
            P(None, "tp"),
            P(),
            P("tp"),
            P("tp"),
            P("tp", None),
            P(),
            P(None, "tp"),
            P(None, "tp"),
            P("tp", None),
        ),
        out_specs=P(("ctx", "tp"), None),
        check_vma=False,
    )
```
